32 devices in a mesh: row: 2 (over x), col: 4 (over z), depth: 4 (over y, core).
Axes of the slice: x: 2, y: 2, z: 4, core: 2. Of those that a mesh axis runs over, the one named last changes fastest.
Arguments:
- tokens: bfloat16 [512, 4096], P(('col', 'depth'), 'row'), may hold values from -72 to 72
- norm_gain: float32 [4096], P('row'), may hold values from 0.25 to 1.75
- w_gate: bfloat16 [4096, 14336], P('row', 'col'), may hold values from -0.09375 to 0.09375
- w_up: bfloat16 [4096, 14336], P('row', 'col'), may hold values from -0.09375 to 0.09375
- w_down: bfloat16 [14336, 4096], P('col', 'row'), may hold values from -0.046875 to 0.046875
- cotangent: bfloat16 [512, 4096], P(('col', 'depth'), 'row'), may hold values from -1.5 to 1.5
Outputs:
- output: bfloat16 [512, 4096], P(('col', 'depth'), 'row')
- grad_tokens: bfloat16 [512, 4096], P(('col', 'depth'), 'row')
- grad_gain: float32 [4096], P('row')
- grad_gate: bfloat16 [4096, 14336], P('row', 'col')
- grad_up: bfloat16 [4096, 14336], P('row', 'col')
- grad_down: bfloat16 [14336, 4096], P('col', 'row')
The draws below stay inside these ranges and needn't reach their ends.
All inputs are finite; a program needn't handle non-finite values.
Results may differ from the reference program's by a relative error of at most 0.023.
Values may be sent and summed in bfloat16 or wider, within the bound.
A program may use at most 192 MiB of HBM per device.

```python
import jax
import jax.numpy as jnp
from jax import lax

D = 4096
FF = 14336
TOK_DEV = 32
TOKENS = 512
N_ROW = 2
N_COL = 4
N_DEPTH = 4


def draw_tokens(key, part):
    key_base, key_cols, key_rows = jax.random.split(jax.random.fold_in(key, 7), 3)
    feature = jnp.arange(D, dtype=jnp.float32) / D - 0.5
    position = jnp.arange(TOKENS, dtype=jnp.float32) / TOKENS
    row_scale = 0.5 * jnp.exp(1.1 * position + jax.random.uniform(key_rows, (TOKENS,), jnp.float32, -0.8, 0.8))
    col_scale = jnp.exp(1.7 * feature + jax.random.uniform(key_cols, (D,), jnp.float32, -0.8, 0.8))
    base = jax.random.truncated_normal(key_base, -4.0, 4.0, (TOKENS, D), jnp.float32)
    return (base * row_scale[:, None] * col_scale[None, :]).astype(jnp.bfloat16)


def block_scale(stream_key, shape, cuts, least, top_value):
    loudness, own = 1.0, jax.random.fold_in(stream_key, 6)
    for axis_at, blocks in cuts:
        heights = jnp.exp(jax.random.uniform(jax.random.fold_in(own, axis_at), (blocks,), jnp.float32, least / len(cuts), top_value / len(cuts)))
        loudness = loudness * jnp.repeat(heights, shape[axis_at] // blocks).reshape([-1 if axis == axis_at else 1 for axis in range(len(shape))])
    return loudness


def scatter_about(stream_key, extent, deviation, bound, pieces=(), kind=jnp.bfloat16):
    values = deviation * jax.random.normal(stream_key, extent, jnp.float32)
    if pieces:
        values = values * block_scale(stream_key, extent, pieces, -0.22, 0.18)
    return jnp.clip(values, -bound, bound).astype(kind)


def setup_inputs(seed: int = 0) -> dict:
    arg_keys = jax.random.split(jax.random.key(seed), 7)
    return {
        "tokens": draw_tokens(jax.random.fold_in(arg_keys[6], 71), 0),
        "norm_gain": jnp.clip(1.0 + 0.15 * jax.random.normal(arg_keys[1], (D,), jnp.float32), 0.25, 1.75),
        "w_gate": scatter_about(arg_keys[2], (D, FF), D ** -0.5, 0.09375, ((0, 2), (1, 4))),
        "w_up": scatter_about(arg_keys[3], (D, FF), D ** -0.5, 0.09375, ((0, 2), (1, 4))),
        "w_down": scatter_about(arg_keys[4], (FF, D), FF ** -0.5, 0.046875, ((0, 4), (1, 2))),
        "cotangent": scatter_about(arg_keys[5], (TOKENS, D), 0.25, 1.5, ((0, 16), (1, 2))),
    }


EPS = 1e-05

def rounded(value):
    low = lax.optimization_barrier(value.astype(jnp.bfloat16))
    return low.astype(jnp.float32)

def block_sum(left, right, parts):
    size = left.shape[1] // parts
    total = jnp.zeros((left.shape[0], right.shape[1]), jnp.float32)
    for index in range(parts):
        piece = jnp.dot(left[:, index * size:(index + 1) * size], right[index * size:(index + 1) * size], preferred_element_type=jnp.float32)
        total = total + rounded(piece)
    return total

def group_rows(array, group):
    shaped = array.reshape(N_COL, N_DEPTH, TOK_DEV, array.shape[1])
    return shaped[:, group].reshape(N_COL * TOK_DEV, array.shape[1])

def reference(tokens, norm_gain, w_gate, w_up, w_down, cotangent):
    inputs = tokens.astype(jnp.float32)
    inv_rms = lax.rsqrt(lax.optimization_barrier(jnp.sum(inputs * inputs, axis=1, keepdims=True)) / D + EPS)
    normal_rows = inputs * inv_rms
    normed = (normal_rows * norm_gain[None, :]).astype(jnp.bfloat16)
    gate = block_sum(normed, w_gate, N_ROW)
    up = block_sum(normed, w_up, N_ROW)
    sig = jax.nn.sigmoid(gate)
    act = gate * sig
    hidden = (act * up).astype(jnp.bfloat16)
    mixed = block_sum(hidden, w_down, N_COL)
    output = (inputs + mixed).astype(jnp.bfloat16)
    grad_hidden = block_sum(cotangent, w_down.T, N_ROW)
    grad_up_h = (grad_hidden * act).astype(jnp.bfloat16)
    grad_gate_h = (grad_hidden * up * sig * (1.0 + gate * (1.0 - sig))).astype(jnp.bfloat16)
    size = FF // N_COL
    grad_normed = jnp.zeros((TOKENS, D), jnp.float32)
    for index in range(N_COL):
        cols = slice(index * size, (index + 1) * size)
        piece = jnp.dot(grad_gate_h[:, cols], w_gate[:, cols].T, preferred_element_type=jnp.float32)
        piece = piece + jnp.dot(grad_up_h[:, cols], w_up[:, cols].T, preferred_element_type=jnp.float32)
        grad_normed = grad_normed + rounded(piece)
    grad_scaled = grad_normed * norm_gain[None, :]
    proj = lax.optimization_barrier(jnp.sum(grad_scaled * normal_rows, axis=1, keepdims=True))
    grad_tokens = (cotangent.astype(jnp.float32) + inv_rms * (grad_scaled - normal_rows * proj / D)).astype(jnp.bfloat16)
    grad_gain = lax.optimization_barrier(jnp.sum(grad_normed * normal_rows, axis=0))
    sum_gate = jnp.zeros((D, FF), jnp.float32)
    sum_up = jnp.zeros((D, FF), jnp.float32)
    sum_down = jnp.zeros((FF, D), jnp.float32)
    for group in range(N_DEPTH):
        normed_g = group_rows(normed, group)
        sum_gate = sum_gate + rounded(jnp.dot(normed_g.T, group_rows(grad_gate_h, group), preferred_element_type=jnp.float32))
        sum_up = sum_up + rounded(jnp.dot(normed_g.T, group_rows(grad_up_h, group), preferred_element_type=jnp.float32))
        sum_down = sum_down + rounded(jnp.dot(group_rows(hidden, group).T, group_rows(cotangent, group), preferred_element_type=jnp.float32))
    return (output, grad_tokens, grad_gain, sum_gate.astype(jnp.bfloat16), sum_up.astype(jnp.bfloat16), sum_down.astype(jnp.bfloat16))
```

```python
import jax
import jax.numpy as jnp
from jax import lax
from jax.sharding import PartitionSpec as P

EPS = 1e-05
BF = jnp.bfloat16
F32 = jnp.float32


def contract_rows(left, right):
    return lax.dot_general(left, right, (((0,), (0,)), ((), ())), preferred_element_type=F32)


def contract_cols(left, right):
    return lax.dot_general(left, right, (((1,), (1,)), ((), ())), preferred_element_type=F32)


def make_body(mesh):
    n_row = mesh.shape["row"]

    def row_total(value):
        if n_row == 2:
            return value.astype(F32) + lax.ppermute(value, "row", [(0, 1), (1, 0)]).astype(F32)
        return lax.psum(value, "row").astype(F32)

    def body(tokens, norm_gain, w_gate, w_up, w_down, cotangent):
        width = tokens.shape[1] * n_row
        inputs = tokens.astype(F32)
        cot_mine = lax.all_gather(cotangent, "col", axis=0, tiled=True)
        sumsq = row_total(jnp.sum(inputs * inputs, axis=1, keepdims=True))
        inv_rms = lax.rsqrt(sumsq / width + EPS)
        normal_rows = inputs * inv_rms
        normed = (normal_rows * norm_gain[None, :]).astype(BF)
        normed_mine = lax.all_gather(normed, "col", axis=0, tiled=True)
        cot_all = lax.all_gather(cot_mine, "depth", axis=0, tiled=True)
        normed_all = lax.all_gather(normed_mine, "depth", axis=0, tiled=True)
        hidden_cols = w_gate.shape[1]
        chunks = 4 if hidden_cols % 512 == 0 else 1
        size = hidden_cols // chunks
        mixed = 0.0
        grad_normed = 0.0
        gates, ups, downs = [], [], []
        parts = []
        for index in range(chunks):
            cols = slice(index * size, (index + 1) * size)
            wg, wu, wd = w_gate[:, cols], w_up[:, cols], w_down[cols, :]
            parts.append(jnp.concatenate(
                [
                    jnp.dot(normed_mine, wg, preferred_element_type=F32).astype(BF),
                    jnp.dot(normed_mine, wu, preferred_element_type=F32).astype(BF),
                    contract_cols(cot_mine, wd).astype(BF),
                ],
                axis=1,
            ))
        trios = []
        for index in range(chunks):
            cols = slice(index * size, (index + 1) * size)
            wg, wu, wd = w_gate[:, cols], w_up[:, cols], w_down[cols, :]
            whole = row_total(parts[index])
            gate, up, grad_hidden = whole[:, :size], whole[:, size:2 * size], whole[:, 2 * size:]
            sig = jax.nn.sigmoid(gate)
            act = gate * sig
            hidden = (act * up).astype(BF)
            grad_up_h = (grad_hidden * act).astype(BF)
            grad_gate_h = (grad_hidden * up * sig * (1.0 + gate * (1.0 - sig))).astype(BF)
            trio = jnp.concatenate([grad_gate_h, grad_up_h, hidden], axis=1)
            trios.append(lax.all_gather(trio, "depth", axis=0, tiled=True))
            mixed = mixed + jnp.dot(hidden, wd, preferred_element_type=F32)
            grad_normed = grad_normed + contract_cols(grad_gate_h, wg) + contract_cols(grad_up_h, wu)
        for trio_all in trios:
            gates.append(contract_rows(normed_all, trio_all[:, :size]).astype(BF))
            ups.append(contract_rows(normed_all, trio_all[:, size:2 * size]).astype(BF))
            downs.append(contract_rows(trio_all[:, 2 * size:], cot_all).astype(BF))
        mixed = lax.psum_scatter(mixed.astype(BF), "col", scatter_dimension=0, tiled=True).astype(F32)
        output = (inputs + mixed).astype(BF)
        grad_normed = lax.psum_scatter(
            grad_normed.astype(BF), "col", scatter_dimension=0, tiled=True
        ).astype(F32)
        grad_scaled = grad_normed * norm_gain[None, :]
        proj = row_total(jnp.sum(grad_scaled * normal_rows, axis=1, keepdims=True))
        grad_tokens = (
            cotangent.astype(F32) + inv_rms * (grad_scaled - normal_rows * (proj / width))
        ).astype(BF)
        grad_gain = lax.psum(jnp.sum(grad_normed * normal_rows, axis=0), ("col", "depth"))
        return (
            output,
            grad_tokens,
            grad_gain,
            jnp.concatenate(gates, axis=1),
            jnp.concatenate(ups, axis=1),
            jnp.concatenate(downs, axis=0),
        )

    return body


def solution(mesh):
    in_specs = (
        P(("col", "depth"), "row"),
        P("row"),
        P("row", "col"),
        P("row", "col"),
        P("col", "row"),
        P(("col", "depth"), "row"),
    )
    out_specs = (
        P(("col", "depth"), "row"),
        P(("col", "depth"), "row"),
        P("row"),
        P("row", "col"),
        P("row", "col"),
        P("col", "row"),
    )
    return jax.shard_map(
        make_body(mesh), mesh=mesh, in_specs=in_specs, out_specs=out_specs, check_vma=False
    )
```

```python
import functools

import jax
import jax.numpy as jnp
from jax import lax
from jax.experimental import pallas as pl
from jax.experimental.pallas import tpu as pltpu
from jax.sharding import PartitionSpec as P

EPS = 1e-05
BF = jnp.bfloat16
F32 = jnp.float32


def contract_rows(left, right):
    return lax.dot_general(left, right, (((0,), (0,)), ((), ())), preferred_element_type=F32)


def contract_cols(left, right):
    return lax.dot_general(left, right, (((1,), (1,)), ((), ())), preferred_element_type=F32)


def make_body(mesh):
    n_row = mesh.shape["row"]

    def row_total(value):
        if n_row == 2:
            return value.astype(F32) + lax.ppermute(value, "row", [(0, 1), (1, 0)]).astype(F32)
        return lax.psum(value, "row").astype(F32)

    def body(tokens, norm_gain, w_gate, w_up, w_down, cotangent):
        width = tokens.shape[1] * n_row
        inputs = tokens.astype(F32)
        cot_mine = lax.all_gather(cotangent, "col", axis=0, tiled=True)
        sumsq = row_total(jnp.sum(inputs * inputs, axis=1, keepdims=True))
        inv_rms = lax.rsqrt(sumsq / width + EPS)
        normal_rows = inputs * inv_rms
        normed = (normal_rows * norm_gain[None, :]).astype(BF)
        normed_mine = lax.all_gather(normed, "col", axis=0, tiled=True)
        cot_all = lax.all_gather(cot_mine, "depth", axis=0, tiled=True)
        normed_all = lax.all_gather(normed_mine, "depth", axis=0, tiled=True)
        hidden_cols = w_gate.shape[1]
        chunks = 4 if hidden_cols % 512 == 0 else 1
        size = hidden_cols // chunks
        mixed = 0.0
        grad_normed = 0.0
        gates, ups, downs = [], [], []
        parts = []
        for index in range(chunks):
            cols = slice(index * size, (index + 1) * size)
            wg, wu, wd = w_gate[:, cols], w_up[:, cols], w_down[cols, :]
            parts.append(jnp.concatenate(
                [
                    jnp.dot(normed_mine, wg, preferred_element_type=F32).astype(BF),
                    jnp.dot(normed_mine, wu, preferred_element_type=F32).astype(BF),
                    contract_cols(cot_mine, wd).astype(BF),
                ],
                axis=1,
            ))
        trios = []
        for index in range(chunks):
            cols = slice(index * size, (index + 1) * size)
            wg, wu, wd = w_gate[:, cols], w_up[:, cols], w_down[cols, :]
            whole = row_total(parts[index])
            gate, up, grad_hidden = whole[:, :size], whole[:, size:2 * size], whole[:, 2 * size:]
            sig = jax.nn.sigmoid(gate)
            act = gate * sig
            hidden = (act * up).astype(BF)
            grad_up_h = (grad_hidden * act).astype(BF)
            grad_gate_h = (grad_hidden * up * sig * (1.0 + gate * (1.0 - sig))).astype(BF)
            trio = jnp.concatenate([grad_gate_h, grad_up_h, hidden], axis=1)
            trios.append(lax.all_gather(trio, "depth", axis=0, tiled=True))
            mixed = mixed + jnp.dot(hidden, wd, preferred_element_type=F32)
            grad_normed = grad_normed + contract_cols(grad_gate_h, wg) + contract_cols(grad_up_h, wu)
        for trio_all in trios:
            gates.append(contract_rows(normed_all, trio_all[:, :size]).astype(BF))
            ups.append(contract_rows(normed_all, trio_all[:, size:2 * size]).astype(BF))
            downs.append(contract_rows(trio_all[:, 2 * size:], cot_all).astype(BF))
        mixed = lax.psum_scatter(mixed.astype(BF), "col", scatter_dimension=0, tiled=True).astype(F32)
        output = (inputs + mixed).astype(BF)
        grad_normed = lax.psum_scatter(
            grad_normed.astype(BF), "col", scatter_dimension=0, tiled=True
        ).astype(F32)
        grad_scaled = grad_normed * norm_gain[None, :]
        proj = row_total(jnp.sum(grad_scaled * normal_rows, axis=1, keepdims=True))
        grad_tokens = (
            cotangent.astype(F32) + inv_rms * (grad_scaled - normal_rows * (proj / width))
        ).astype(BF)
        grad_gain = lax.psum(jnp.sum(grad_normed * normal_rows, axis=0), ("col", "depth"))
        return (
            output,
            grad_tokens,
            grad_gain,
            jnp.concatenate(gates, axis=1),
            jnp.concatenate(ups, axis=1),
            jnp.concatenate(downs, axis=0),
        )

    return body


MESH = pl.DeviceIdType.MESH


def exchange_kernel(n_col, chunks, size, width, tok_ref, gain_ref, cot_ref, wg_hbm, wu_hbm, wd_hbm,
                    mixed_ref, gn_ref, inv_ref, nall, call, gg_all, gu_all, h_all,
                    wg, wu, wd, mine, sq_out, sq_in, part, peer, trio, acc_m, acc_g,
                    w_sem, sq_sem, ring_send, ring_recv, x_send, x_recv,
                    y_send, y_recv, c_send, c_recv, f_send, f_recv, l_sem,
                    ay_send, ay_recv, ac_send, ac_recv, af_send, af_recv, al_sem):
    row, col, dep = lax.axis_index("row"), lax.axis_index("col"), lax.axis_index("depth")
    x_peer = {"row": 1 - row}
    y_dep = lax.rem(dep + 2, 4)
    y_peer = {"depth": y_dep}
    c_peer = {"depth": dep + 1 - 2 * lax.rem(dep, 2)}
    block = tok_ref.shape[0]
    has_left, has_right = col > 0, col < n_col - 1

    def cols_of(c):
        return pl.ds(pl.multiple_of(c * size, size), size)

    def w_copies(c):
        return (
            pltpu.make_async_copy(wd_hbm.at[cols_of(c), :], wd.at[c], w_sem.at[c, 0]),
            pltpu.make_async_copy(wg_hbm.at[:, cols_of(c)], wg.at[c], w_sem.at[c, 1]),
            pltpu.make_async_copy(wu_hbm.at[:, cols_of(c)], wu.at[c], w_sem.at[c, 2]),
        )

    @pl.loop(0, chunks)
    def _(c):
        for copy in w_copies(c):
            copy.start()

    barrier = pltpu.get_barrier_semaphore()
    for peer_id in (x_peer, y_peer, c_peer):
        pl.semaphore_signal(barrier, inc=1, device_id=peer_id, device_id_type=MESH)

    @pl.when(has_left)
    def _():
        pl.semaphore_signal(barrier, inc=1, device_id={"col": col - 1}, device_id_type=MESH)

    @pl.when(has_right)
    def _():
        pl.semaphore_signal(barrier, inc=1, device_id={"col": col + 1}, device_id_type=MESH)

    own_rows = pl.ds(pl.multiple_of(col * block, block), block)
    mine[1, own_rows, :] = cot_ref[...]
    inputs = tok_ref[...].astype(F32)
    sq_out[...] = jnp.broadcast_to(jnp.sum(inputs * inputs, axis=1, keepdims=True), sq_out.shape)
    pl.semaphore_wait(barrier, 3 + has_left.astype(jnp.int32) + has_right.astype(jnp.int32))
    sq_copy = pltpu.make_async_remote_copy(sq_out, sq_in, sq_sem.at[0], sq_sem.at[1], device_id=x_peer, device_id_type=MESH)
    sq_copy.start()

    def hop(which, step, way):
        origin = col - step if way == 0 else col + step
        target = col + 1 if way == 0 else col - 1
        rows = pl.ds(pl.multiple_of(origin * block, block), block)
        return pltpu.make_async_remote_copy(
            mine.at[which, rows, :], mine.at[which, rows, :],
            ring_send.at[which, step, way], ring_recv.at[which, step, way],
            device_id={"col": target}, device_id_type=MESH)

    def sends(which, step, act):
        @pl.when((col - step >= 0) & has_right)
        def _():
            act(hop(which, step, 0))

        @pl.when((col + step < n_col) & has_left)
        def _():
            act(hop(which, step, 1))

    def arrive(which, step):
        @pl.when(col - 1 - step >= 0)
        def _():
            rows = pl.ds(pl.multiple_of((col - 1 - step) * block, block), block)
            pltpu.make_async_remote_copy(
                mine.at[which, rows, :], mine.at[which, rows, :],
                ring_send.at[which, step, 0], ring_recv.at[which, step, 0],
                device_id={"col": col - 1}, device_id_type=MESH).wait_recv()

        @pl.when(col + 1 + step < n_col)
        def _():
            rows = pl.ds(pl.multiple_of((col + 1 + step) * block, block), block)
            pltpu.make_async_remote_copy(
                mine.at[which, rows, :], mine.at[which, rows, :],
                ring_send.at[which, step, 1], ring_recv.at[which, step, 1],
                device_id={"col": col + 1}, device_id_type=MESH).wait_recv()

    sends(1, 0, lambda copy: copy.start())
    sq_copy.wait()
    inv = lax.rsqrt((sq_out[...] + sq_in[...]) / width + EPS)
    inv_ref[...] = inv
    mine[0, own_rows, :] = (inputs * inv[:, :1] * gain_ref[...]).astype(BF)
    sends(0, 0, lambda copy: copy.start())
    for step in range(n_col - 1):
        for which in (1, 0):
            arrive(which, step)
            if step + 1 < n_col - 1:
                sends(which, step + 1, lambda copy: copy.start())
    for step in range(n_col - 1):
        for which in (1, 0):
            sends(which, step, lambda copy: copy.wait_send())

    def remote(src, dst, a, b, to):
        return pltpu.make_async_remote_copy(src, dst, a, b, device_id=to, device_id_type=MESH)

    def act_copies(which):
        out = (nall, call)[which]
        return (
            remote(mine.at[which], out.at[dep], ay_send.at[which], ay_recv.at[which], y_peer),
            remote(mine.at[which], out.at[dep], ac_send.at[which], ac_recv.at[which], c_peer),
            pltpu.make_async_copy(mine.at[which], out.at[dep], al_sem.at[which]),
        )

    def act_forward(which):
        out = (nall, call)[which]
        return remote(out.at[y_dep], out.at[y_dep], af_send.at[which], af_recv.at[which], c_peer)

    for which in (1, 0):
        for copy in act_copies(which):
            copy.start()

    def x_copy(c):
        return remote(part.at[c], peer.at[c], x_send.at[c], x_recv.at[c], x_peer)

    @pl.loop(0, chunks)
    def _(c):
        for copy in w_copies(c):
            copy.wait()
        part[c, 2] = contract_cols(mine[1], wd[c]).astype(BF)
        part[c, 0] = jnp.dot(mine[0], wg[c], preferred_element_type=F32).astype(BF)
        part[c, 1] = jnp.dot(mine[0], wu[c], preferred_element_type=F32).astype(BF)
        x_copy(c).start()

    outs = (gg_all, gu_all, h_all)

    def spread(c, k):
        dst = outs[k].at[dep, :, cols_of(c)]
        return (
            remote(trio.at[c, k], dst, y_send.at[c, k], y_recv.at[c, k], y_peer),
            remote(trio.at[c, k], dst, c_send.at[c, k], c_recv.at[c, k], c_peer),
            pltpu.make_async_copy(trio.at[c, k], dst, l_sem.at[c, k]),
        )

    def forward(c, k):
        ref = outs[k].at[y_dep, :, cols_of(c)]
        return remote(ref, ref, f_send.at[c, k], f_recv.at[c, k], c_peer)

    def pass_on(c):
        for k in range(3):
            spread(c, k)[0].wait_recv()
            forward(c, k).start()

    acc_m[...] = jnp.zeros_like(acc_m)
    acc_g[...] = jnp.zeros_like(acc_g)
    for which in (1, 0):
        act_copies(which)[0].wait_recv()
        act_forward(which).start()

    @pl.loop(0, chunks)
    def _(c):
        x_copy(c).wait()
        gate = part[c, 0].astype(F32) + peer[c, 0].astype(F32)
        up = part[c, 1].astype(F32) + peer[c, 1].astype(F32)
        grad_hidden = part[c, 2].astype(F32) + peer[c, 2].astype(F32)
        sig = jax.nn.sigmoid(gate)
        act = gate * sig
        trio[c, 2] = (act * up).astype(BF)
        trio[c, 1] = (grad_hidden * act).astype(BF)
        trio[c, 0] = (grad_hidden * up * sig * (1.0 + gate * (1.0 - sig))).astype(BF)
        for k in range(3):
            for copy in spread(c, k):
                copy.start()
        acc_m[...] += jnp.dot(trio[c, 2], wd[c], preferred_element_type=F32)
        acc_g[...] += contract_cols(trio[c, 0], wg[c]) + contract_cols(trio[c, 1], wu[c])

        @pl.when(c > 0)
        def _():
            pass_on(c - 1)

    mixed_ref[...] = acc_m[...].astype(BF)
    gn_ref[...] = acc_g[...].astype(BF)
    pass_on(chunks - 1)
    for which in (1, 0):
        y_one, c_one, l_one = act_copies(which)
        y_one.wait_send()
        c_one.wait()
        l_one.wait()
        act_forward(which).wait()

    @pl.loop(0, chunks)
    def _(c):
        for k in range(3):
            y_one, c_one, l_one = spread(c, k)
            y_one.wait_send()
            c_one.wait()
            l_one.wait()
            forward(c, k).wait()


def exchange(mesh, tokens, norm_gain, cotangent, w_gate, w_up, w_down):
    n_col = mesh.shape["col"]
    block, feat = tokens.shape
    hidden = w_gate.shape[1]
    size = next(s for s in (512, 256, 128) if hidden % s == 0)
    chunks = hidden // size
    rows = block * n_col
    sds = jax.ShapeDtypeStruct
    dma = pltpu.SemaphoreType.DMA
    vmem, hbm = pl.BlockSpec(memory_space=pltpu.VMEM), pl.BlockSpec(memory_space=pl.ANY)
    return pl.pallas_call(
        functools.partial(exchange_kernel, n_col, chunks, size, feat * 2),
        out_shape=[sds((rows, feat), BF)] * 2 + [sds((block, 128), F32)]
        + [sds((4, rows, feat), BF)] * 2 + [sds((4, rows, hidden), BF)] * 3,
        in_specs=[vmem] * 3 + [hbm] * 3,
        out_specs=[vmem] * 3 + [hbm] * 5,
        scratch_shapes=[
            pltpu.VMEM((chunks, feat, size), BF),
            pltpu.VMEM((chunks, feat, size), BF),
            pltpu.VMEM((chunks, size, feat), BF),
            pltpu.VMEM((2, rows, feat), BF),
            pltpu.VMEM((block, 128), F32),
            pltpu.VMEM((block, 128), F32),
            pltpu.VMEM((chunks, 3, rows, size), BF),
            pltpu.VMEM((chunks, 3, rows, size), BF),
            pltpu.VMEM((chunks, 3, rows, size), BF),
            pltpu.VMEM((rows, feat), F32),
            pltpu.VMEM((rows, feat), F32),
            dma((chunks, 3)), dma((2,)), dma((2, n_col, 2)), dma((2, n_col, 2)), dma((chunks,)), dma((chunks,)),
        ] + [dma((chunks, 3))] * 7 + [dma((2,))] * 7,
        compiler_params=pltpu.CompilerParams(
            collective_id=0, has_side_effects=True, vmem_limit_bytes=62 * 1024 * 1024
        ),
        cost_estimate=pl.CostEstimate(
            flops=12 * rows * feat * hidden, bytes_accessed=6 * feat * hidden + 24 * rows * hidden,
            transcendentals=rows * hidden),
    )(tokens, norm_gain[None, :], cotangent, w_gate, w_up, w_down)


def make_fused(mesh):
    n_col = mesh.shape["col"]

    def swap_add(value, axis, bit):
        count = mesh.shape[axis]
        return value + lax.ppermute(value, axis, [(i, i ^ bit) for i in range(count)])

    def body(tokens, norm_gain, w_gate, w_up, w_down, cotangent):
        width = tokens.shape[1] * 2
        mixed, grad_normed, inv, nall, call, gg_all, gu_all, h_all = exchange(
            mesh, tokens, norm_gain, cotangent, w_gate, w_up, w_down)
        mixed, grad_normed = (
            lax.psum_scatter(value, "col", scatter_dimension=0, tiled=True).astype(F32)
            for value in (mixed, grad_normed)
        )
        nall, call, gg_all, gu_all, h_all = (
            value.reshape(-1, value.shape[2]) for value in (nall, call, gg_all, gu_all, h_all))
        grad_gate = contract_rows(nall, gg_all).astype(BF)
        grad_up = contract_rows(nall, gu_all).astype(BF)
        grad_down = contract_rows(h_all, call).astype(BF)
        inputs = tokens.astype(F32)
        inv_rms = inv[:, :1]
        normal_rows = inputs * inv_rms
        output = (inputs + mixed).astype(BF)
        grad_scaled = grad_normed * norm_gain[None, :]
        proj = swap_add(jnp.sum(grad_scaled * normal_rows, axis=1, keepdims=True), "row", 1)
        grad_tokens = (
            cotangent.astype(F32) + inv_rms * (grad_scaled - normal_rows * (proj / width))
        ).astype(BF)
        grad_gain = jnp.sum(grad_normed * normal_rows, axis=0)
        for axis in ("depth", "col"):
            bit = 1
            while bit < mesh.shape[axis]:
                grad_gain = swap_add(grad_gain, axis, bit)
                bit *= 2
        return output, grad_tokens, grad_gain, grad_gate, grad_up, grad_down

    return body


def pick_body(mesh):
    shape = mesh.shape
    if shape["row"] == 2 and shape["depth"] == 4 and shape["col"] == 4:
        return make_fused(mesh)
    return make_body(mesh)


def solution(mesh):
    in_specs = (
        P(("col", "depth"), "row"),
        P("row"),
        P("row", "col"),
        P("row", "col"),
        P("col", "row"),
        P(("col", "depth"), "row"),
    )
    out_specs = (
        P(("col", "depth"), "row"),
        P(("col", "depth"), "row"),
        P("row"),
        P("row", "col"),
        P("row", "col"),
        P("col", "row"),
    )
    return jax.shard_map(
        pick_body(mesh), mesh=mesh, in_specs=in_specs, out_specs=out_specs, check_vma=False
    )
```

```python
import functools

import jax
import jax.numpy as jnp
from jax import lax
from jax.experimental import pallas as pl
from jax.experimental.pallas import tpu as pltpu
from jax.sharding import PartitionSpec as P

EPS = 1e-05
BF = jnp.bfloat16
F32 = jnp.float32


def contract_rows(left, right):
    return lax.dot_general(left, right, (((0,), (0,)), ((), ())), preferred_element_type=F32)


def contract_cols(left, right):
    return lax.dot_general(left, right, (((1,), (1,)), ((), ())), preferred_element_type=F32)


def make_body(mesh):
    n_row = mesh.shape["row"]

    def row_total(value):
        if n_row == 2:
            return value.astype(F32) + lax.ppermute(value, "row", [(0, 1), (1, 0)]).astype(F32)
        return lax.psum(value, "row").astype(F32)

    def body(tokens, norm_gain, w_gate, w_up, w_down, cotangent):
        width = tokens.shape[1] * n_row
        inputs = tokens.astype(F32)
        cot_mine = lax.all_gather(cotangent, "col", axis=0, tiled=True)
        sumsq = row_total(jnp.sum(inputs * inputs, axis=1, keepdims=True))
        inv_rms = lax.rsqrt(sumsq / width + EPS)
        normal_rows = inputs * inv_rms
        normed = (normal_rows * norm_gain[None, :]).astype(BF)
        normed_mine = lax.all_gather(normed, "col", axis=0, tiled=True)
        cot_all = lax.all_gather(cot_mine, "depth", axis=0, tiled=True)
        normed_all = lax.all_gather(normed_mine, "depth", axis=0, tiled=True)
        hidden_cols = w_gate.shape[1]
        chunks = 4 if hidden_cols % 512 == 0 else 1
        size = hidden_cols // chunks
        mixed = 0.0
        grad_normed = 0.0
        gates, ups, downs = [], [], []
        parts = []
        for index in range(chunks):
            cols = slice(index * size, (index + 1) * size)
            wg, wu, wd = w_gate[:, cols], w_up[:, cols], w_down[cols, :]
            parts.append(jnp.concatenate(
                [
                    jnp.dot(normed_mine, wg, preferred_element_type=F32).astype(BF),
                    jnp.dot(normed_mine, wu, preferred_element_type=F32).astype(BF),
                    contract_cols(cot_mine, wd).astype(BF),
                ],
                axis=1,
            ))
        trios = []
        for index in range(chunks):
            cols = slice(index * size, (index + 1) * size)
            wg, wu, wd = w_gate[:, cols], w_up[:, cols], w_down[cols, :]
            whole = row_total(parts[index])
            gate, up, grad_hidden = whole[:, :size], whole[:, size:2 * size], whole[:, 2 * size:]
            sig = jax.nn.sigmoid(gate)
            act = gate * sig
            hidden = (act * up).astype(BF)
            grad_up_h = (grad_hidden * act).astype(BF)
            grad_gate_h = (grad_hidden * up * sig * (1.0 + gate * (1.0 - sig))).astype(BF)
            trio = jnp.concatenate([grad_gate_h, grad_up_h, hidden], axis=1)
            trios.append(lax.all_gather(trio, "depth", axis=0, tiled=True))
            mixed = mixed + jnp.dot(hidden, wd, preferred_element_type=F32)
            grad_normed = grad_normed + contract_cols(grad_gate_h, wg) + contract_cols(grad_up_h, wu)
        for trio_all in trios:
            gates.append(contract_rows(normed_all, trio_all[:, :size]).astype(BF))
            ups.append(contract_rows(normed_all, trio_all[:, size:2 * size]).astype(BF))
            downs.append(contract_rows(trio_all[:, 2 * size:], cot_all).astype(BF))
        mixed = lax.psum_scatter(mixed.astype(BF), "col", scatter_dimension=0, tiled=True).astype(F32)
        output = (inputs + mixed).astype(BF)
        grad_normed = lax.psum_scatter(
            grad_normed.astype(BF), "col", scatter_dimension=0, tiled=True
        ).astype(F32)
        grad_scaled = grad_normed * norm_gain[None, :]
        proj = row_total(jnp.sum(grad_scaled * normal_rows, axis=1, keepdims=True))
        grad_tokens = (
            cotangent.astype(F32) + inv_rms * (grad_scaled - normal_rows * (proj / width))
        ).astype(BF)
        grad_gain = lax.psum(jnp.sum(grad_normed * normal_rows, axis=0), ("col", "depth"))
        return (
            output,
            grad_tokens,
            grad_gain,
            jnp.concatenate(gates, axis=1),
            jnp.concatenate(ups, axis=1),
            jnp.concatenate(downs, axis=0),
        )

    return body


MESH = pl.DeviceIdType.MESH


def exchange_kernel(n_col, chunks, size, width, tok_ref, gain_ref, cot_ref, wg_hbm, wu_hbm, wd_hbm,
                    mixed_ref, gn_ref, inv_ref, nall, call, gg_all, gu_all, h_all,
                    wg, wu, wd, both, sq_out, sq_in, part, peer, trio, acc_m, acc_g, end_out, end_in,
                    w_sem, sq_sem, ring_send, ring_recv, x_send, x_recv,
                    y_send, y_recv, c_send, c_recv, f_send, f_recv, l_sem,
                    ay_send, ay_recv, ac_send, ac_recv, af_send, af_recv, al_sem, e_send, e_recv):
    row, col, dep = lax.axis_index("row"), lax.axis_index("col"), lax.axis_index("depth")
    x_peer = {"row": 1 - row}
    me = lax.rem(dep, 2)
    y_peer = {"depth": lax.rem(dep + 2, 4)}
    c_peer = {"depth": dep + 1 - 2 * me}
    chip = pl.ds(dep - me, 2)
    y_chip = pl.ds(lax.rem(dep - me + 2, 4), 2)
    block = tok_ref.shape[0]
    has_left, has_right = col > 0, col < n_col - 1

    def cols_of(c):
        return pl.ds(pl.multiple_of((me * chunks + c) * size, size), size)

    def w_copies(c):
        return (
            pltpu.make_async_copy(wd_hbm.at[cols_of(c), :], wd.at[c], w_sem.at[c, 0]),
            pltpu.make_async_copy(wg_hbm.at[:, cols_of(c)], wg.at[c], w_sem.at[c, 1]),
            pltpu.make_async_copy(wu_hbm.at[:, cols_of(c)], wu.at[c], w_sem.at[c, 2]),
        )

    @pl.loop(0, chunks)
    def _(c):
        for copy in w_copies(c):
            copy.start()

    barrier = pltpu.get_barrier_semaphore()
    for peer_id in (x_peer, y_peer, c_peer):
        pl.semaphore_signal(barrier, inc=1, device_id=peer_id, device_id_type=MESH)

    @pl.when(has_left)
    def _():
        pl.semaphore_signal(barrier, inc=1, device_id={"col": col - 1}, device_id_type=MESH)

    @pl.when(has_right)
    def _():
        pl.semaphore_signal(barrier, inc=1, device_id={"col": col + 1}, device_id_type=MESH)

    own_rows = pl.ds(pl.multiple_of(col * block, block), block)
    both[1, me, own_rows, :] = cot_ref[...]
    inputs = tok_ref[...].astype(F32)
    sq_out[...] = jnp.broadcast_to(jnp.sum(inputs * inputs, axis=1, keepdims=True), sq_out.shape)
    pl.semaphore_wait(barrier, 3 + has_left.astype(jnp.int32) + has_right.astype(jnp.int32))
    sq_copy = pltpu.make_async_remote_copy(sq_out, sq_in, sq_sem.at[0], sq_sem.at[1], device_id=x_peer, device_id_type=MESH)
    sq_copy.start()

    def hop(which, step, way):
        origin = col - step if way == 0 else col + step
        target = col + 1 if way == 0 else col - 1
        rows = pl.ds(pl.multiple_of(origin * block, block), block)
        return pltpu.make_async_remote_copy(
            both.at[which, me, rows, :], both.at[which, me, rows, :],
            ring_send.at[which, step, way], ring_recv.at[which, step, way],
            device_id={"col": target}, device_id_type=MESH)

    def sends(which, step, act):
        @pl.when((col - step >= 0) & has_right)
        def _():
            act(hop(which, step, 0))

        @pl.when((col + step < n_col) & has_left)
        def _():
            act(hop(which, step, 1))

    def arrive(which, step):
        @pl.when(col - 1 - step >= 0)
        def _():
            rows = pl.ds(pl.multiple_of((col - 1 - step) * block, block), block)
            pltpu.make_async_remote_copy(
                both.at[which, me, rows, :], both.at[which, me, rows, :],
                ring_send.at[which, step, 0], ring_recv.at[which, step, 0],
                device_id={"col": col - 1}, device_id_type=MESH).wait_recv()

        @pl.when(col + 1 + step < n_col)
        def _():
            rows = pl.ds(pl.multiple_of((col + 1 + step) * block, block), block)
            pltpu.make_async_remote_copy(
                both.at[which, me, rows, :], both.at[which, me, rows, :],
                ring_send.at[which, step, 1], ring_recv.at[which, step, 1],
                device_id={"col": col + 1}, device_id_type=MESH).wait_recv()

    sends(1, 0, lambda copy: copy.start())
    sq_copy.wait()
    inv = lax.rsqrt((sq_out[...] + sq_in[...]) / width + EPS)
    inv_ref[...] = inv
    both[0, me, own_rows, :] = (inputs * inv[:, :1] * gain_ref[...]).astype(BF)
    sends(0, 0, lambda copy: copy.start())
    for step in range(n_col - 1):
        for which in (1, 0):
            arrive(which, step)
            if step + 1 < n_col - 1:
                sends(which, step + 1, lambda copy: copy.start())
    for step in range(n_col - 1):
        for which in (1, 0):
            sends(which, step, lambda copy: copy.wait_send())

    def remote(src, dst, a, b, to):
        return pltpu.make_async_remote_copy(src, dst, a, b, device_id=to, device_id_type=MESH)

    def y_act(which):
        out = (nall, call)[which]
        return remote(both.at[which, me], out.at[dep], ay_send.at[which], ay_recv.at[which], y_peer)

    def c_act(which):
        return remote(both.at[which, me], both.at[which, me], ac_send.at[which], ac_recv.at[which], c_peer)

    def own_act(which):
        return pltpu.make_async_copy(both.at[which], (nall, call)[which].at[chip], al_sem.at[which])

    def act_forward(which):
        ref = (nall, call)[which].at[lax.rem(dep + 2, 4)]
        return remote(ref, ref, af_send.at[which], af_recv.at[which], c_peer)

    for which in (1, 0):
        c_act(which).start()
        y_act(which).start()
    for which in (1, 0):
        c_act(which).wait()
        own_act(which).start()

    def x_copy(c):
        return remote(part.at[c], peer.at[c], x_send.at[c], x_recv.at[c], x_peer)

    @pl.loop(0, chunks)
    def _(c):
        for copy in w_copies(c):
            copy.wait()
        cot_rows = both[1].reshape(-1, both.shape[3])
        norm_rows = both[0].reshape(-1, both.shape[3])
        shape = part.shape[2:]
        part[c, 2] = contract_cols(cot_rows, wd[c]).astype(BF).reshape(shape)
        part[c, 0] = jnp.dot(norm_rows, wg[c], preferred_element_type=F32).astype(BF).reshape(shape)
        part[c, 1] = jnp.dot(norm_rows, wu[c], preferred_element_type=F32).astype(BF).reshape(shape)
        x_copy(c).start()

    outs = (gg_all, gu_all, h_all)

    def spread(c, k):
        dst = outs[k].at[chip, :, cols_of(c)]
        return (
            remote(trio.at[c, k], dst, y_send.at[c, k], y_recv.at[c, k], y_peer),
            remote(trio.at[c, k], dst, c_send.at[c, k], c_recv.at[c, k], c_peer),
            pltpu.make_async_copy(trio.at[c, k], dst, l_sem.at[c, k]),
        )

    def forward(c, k):
        ref = outs[k].at[y_chip, :, cols_of(c)]
        return remote(ref, ref, f_send.at[c, k], f_recv.at[c, k], c_peer)

    def pass_on(c):
        for k in range(3):
            spread(c, k)[0].wait_recv()
            forward(c, k).start()

    acc_m[...] = jnp.zeros_like(acc_m)
    acc_g[...] = jnp.zeros_like(acc_g)
    for which in (1, 0):
        y_act(which).wait_recv()
        act_forward(which).start()

    @pl.loop(0, chunks)
    def _(c):
        x_copy(c).wait()
        gate = part[c, 0].astype(F32) + peer[c, 0].astype(F32)
        up = part[c, 1].astype(F32) + peer[c, 1].astype(F32)
        grad_hidden = part[c, 2].astype(F32) + peer[c, 2].astype(F32)
        sig = jax.nn.sigmoid(gate)
        act = gate * sig
        trio[c, 2] = (act * up).astype(BF)
        trio[c, 1] = (grad_hidden * act).astype(BF)
        trio[c, 0] = (grad_hidden * up * sig * (1.0 + gate * (1.0 - sig))).astype(BF)
        for k in range(3):
            for copy in spread(c, k):
                copy.start()
        flat = [trio[c, k].reshape(-1, size) for k in range(3)]
        shape = acc_m.shape
        acc_m[...] += jnp.dot(flat[2], wd[c], preferred_element_type=F32).reshape(shape)
        acc_g[...] += (contract_cols(flat[0], wg[c]) + contract_cols(flat[1], wu[c])).reshape(shape)

        @pl.when(c > 0)
        def _():
            pass_on(c - 1)

    def end_copy(k):
        return remote(end_out.at[k], end_in.at[k], e_send.at[k], e_recv.at[k], c_peer)

    end_out[0] = acc_m[1 - me].astype(BF)
    end_copy(0).start()
    end_out[1] = acc_g[1 - me].astype(BF)
    end_copy(1).start()
    pass_on(chunks - 1)
    for which in (1, 0):
        y_act(which).wait_send()
        own_act(which).wait()
        act_forward(which).wait()
    end_copy(0).wait()
    mixed_ref[...] = (acc_m[me] + end_in[0].astype(F32)).astype(BF)
    end_copy(1).wait()
    gn_ref[...] = (acc_g[me] + end_in[1].astype(F32)).astype(BF)

    @pl.loop(0, chunks)
    def _(c):
        for k in range(3):
            y_one, c_one, l_one = spread(c, k)
            y_one.wait_send()
            c_one.wait()
            l_one.wait()
            forward(c, k).wait()


def exchange(mesh, tokens, norm_gain, cotangent, w_gate, w_up, w_down):
    n_col = mesh.shape["col"]
    block, feat = tokens.shape
    hidden = w_gate.shape[1]
    size = next(s for s in (256, 128) if hidden % (2 * s) == 0)
    chunks = hidden // (2 * size)
    rows = block * n_col
    sds = jax.ShapeDtypeStruct
    dma = pltpu.SemaphoreType.DMA
    vmem, hbm = pl.BlockSpec(memory_space=pltpu.VMEM), pl.BlockSpec(memory_space=pl.ANY)
    return pl.pallas_call(
        functools.partial(exchange_kernel, n_col, chunks, size, feat * 2),
        out_shape=[sds((rows, feat), BF)] * 2 + [sds((block, 128), F32)]
        + [sds((4, rows, feat), BF)] * 2 + [sds((4, rows, hidden), BF)] * 3,
        in_specs=[vmem] * 3 + [hbm] * 3,
        out_specs=[vmem] * 3 + [hbm] * 5,
        scratch_shapes=[
            pltpu.VMEM((chunks, feat, size), BF),
            pltpu.VMEM((chunks, feat, size), BF),
            pltpu.VMEM((chunks, size, feat), BF),
            pltpu.VMEM((2, 2, rows, feat), BF),
            pltpu.VMEM((block, 128), F32),
            pltpu.VMEM((block, 128), F32),
            pltpu.VMEM((chunks, 3, 2, rows, size), BF),
            pltpu.VMEM((chunks, 3, 2, rows, size), BF),
            pltpu.VMEM((chunks, 3, 2, rows, size), BF),
            pltpu.VMEM((2, rows, feat), F32),
            pltpu.VMEM((2, rows, feat), F32),
            pltpu.VMEM((2, rows, feat), BF),
            pltpu.VMEM((2, rows, feat), BF),
            dma((chunks, 3)), dma((2,)), dma((2, n_col, 2)), dma((2, n_col, 2)), dma((chunks,)), dma((chunks,)),
        ] + [dma((chunks, 3))] * 7 + [dma((2,))] * 9,
        compiler_params=pltpu.CompilerParams(
            collective_id=0, has_side_effects=True, vmem_limit_bytes=62 * 1024 * 1024
        ),
        cost_estimate=pl.CostEstimate(
            flops=12 * rows * feat * hidden, bytes_accessed=6 * feat * hidden + 24 * rows * hidden,
            transcendentals=rows * hidden),
    )(tokens, norm_gain[None, :], cotangent, w_gate, w_up, w_down)


def make_fused(mesh):
    n_col = mesh.shape["col"]

    def swap_add(value, axis, bit):
        count = mesh.shape[axis]
        return value + lax.ppermute(value, axis, [(i, i ^ bit) for i in range(count)])

    def body(tokens, norm_gain, w_gate, w_up, w_down, cotangent):
        width = tokens.shape[1] * 2
        mixed, grad_normed, inv, nall, call, gg_all, gu_all, h_all = exchange(
            mesh, tokens, norm_gain, cotangent, w_gate, w_up, w_down)
        mixed, grad_normed = (
            lax.psum_scatter(value, "col", scatter_dimension=0, tiled=True).astype(F32)
            for value in (mixed, grad_normed)
        )
        nall, call, gg_all, gu_all, h_all = (
            value.reshape(-1, value.shape[2]) for value in (nall, call, gg_all, gu_all, h_all))
        grad_gate = contract_rows(nall, gg_all).astype(BF)
        grad_up = contract_rows(nall, gu_all).astype(BF)
        mixed, grad_normed, grad_gate, grad_up, h_all, call = lax.optimization_barrier(
            (mixed, grad_normed, grad_gate, grad_up, h_all, call))
        grad_down = contract_rows(h_all, call).astype(BF)
        inputs = tokens.astype(F32)
        inv_rms = inv[:, :1]
        normal_rows = inputs * inv_rms
        output = (inputs + mixed).astype(BF)
        grad_scaled = grad_normed * norm_gain[None, :]
        proj = swap_add(jnp.sum(grad_scaled * normal_rows, axis=1, keepdims=True), "row", 1)
        grad_tokens = (
            cotangent.astype(F32) + inv_rms * (grad_scaled - normal_rows * (proj / width))
        ).astype(BF)
        grad_gain = jnp.sum(grad_normed * normal_rows, axis=0)
        for axis in ("depth", "col"):
            count = mesh.shape[axis]
            grad_gain = grad_gain + sum(
                lax.ppermute(grad_gain, axis, [(i, (i + step) % count) for i in range(count)])
                for step in range(1, count))
        return output, grad_tokens, grad_gain, grad_gate, grad_up, grad_down

    return body


def pick_body(mesh):
    shape = mesh.shape
    if shape["row"] == 2 and shape["depth"] == 4 and shape["col"] == 4:
        return make_fused(mesh)
    return make_body(mesh)


def solution(mesh):
    in_specs = (
        P(("col", "depth"), "row"),
        P("row"),
        P("row", "col"),
        P("row", "col"),
        P("col", "row"),
        P(("col", "depth"), "row"),
    )
    out_specs = (
        P(("col", "depth"), "row"),
        P(("col", "depth"), "row"),
        P("row"),
        P("row", "col"),
        P("row", "col"),
        P("col", "row"),
    )
    return jax.shard_map(
        pick_body(mesh), mesh=mesh, in_specs=in_specs, out_specs=out_specs, check_vma=False
    )
```

```python
import functools

import jax
import jax.numpy as jnp
from jax import lax
from jax.experimental import pallas as pl
from jax.experimental.pallas import tpu as pltpu
from jax.sharding import PartitionSpec as P

EPS = 1e-05
BF = jnp.bfloat16
F32 = jnp.float32


def contract_rows(left, right):
    return lax.dot_general(left, right, (((0,), (0,)), ((), ())), preferred_element_type=F32)


def contract_cols(left, right):
    return lax.dot_general(left, right, (((1,), (1,)), ((), ())), preferred_element_type=F32)


def make_body(mesh):
    n_row = mesh.shape["row"]

    def row_total(value):
        if n_row == 2:
            return value.astype(F32) + lax.ppermute(value, "row", [(0, 1), (1, 0)]).astype(F32)
        return lax.psum(value, "row").astype(F32)

    def body(tokens, norm_gain, w_gate, w_up, w_down, cotangent):
        width = tokens.shape[1] * n_row
        inputs = tokens.astype(F32)
        cot_mine = lax.all_gather(cotangent, "col", axis=0, tiled=True)
        sumsq = row_total(jnp.sum(inputs * inputs, axis=1, keepdims=True))
        inv_rms = lax.rsqrt(sumsq / width + EPS)
        normal_rows = inputs * inv_rms
        normed = (normal_rows * norm_gain[None, :]).astype(BF)
        normed_mine = lax.all_gather(normed, "col", axis=0, tiled=True)
        cot_all = lax.all_gather(cot_mine, "depth", axis=0, tiled=True)
        normed_all = lax.all_gather(normed_mine, "depth", axis=0, tiled=True)
        hidden_cols = w_gate.shape[1]
        chunks = 4 if hidden_cols % 512 == 0 else 1
        size = hidden_cols // chunks
        mixed = 0.0
        grad_normed = 0.0
        gates, ups, downs = [], [], []
        parts = []
        for index in range(chunks):
            cols = slice(index * size, (index + 1) * size)
            wg, wu, wd = w_gate[:, cols], w_up[:, cols], w_down[cols, :]
            parts.append(jnp.concatenate(
                [
                    jnp.dot(normed_mine, wg, preferred_element_type=F32).astype(BF),
                    jnp.dot(normed_mine, wu, preferred_element_type=F32).astype(BF),
                    contract_cols(cot_mine, wd).astype(BF),
                ],
                axis=1,
            ))
        trios = []
        for index in range(chunks):
            cols = slice(index * size, (index + 1) * size)
            wg, wu, wd = w_gate[:, cols], w_up[:, cols], w_down[cols, :]
            whole = row_total(parts[index])
            gate, up, grad_hidden = whole[:, :size], whole[:, size:2 * size], whole[:, 2 * size:]
            sig = jax.nn.sigmoid(gate)
            act = gate * sig
            hidden = (act * up).astype(BF)
            grad_up_h = (grad_hidden * act).astype(BF)
            grad_gate_h = (grad_hidden * up * sig * (1.0 + gate * (1.0 - sig))).astype(BF)
            trio = jnp.concatenate([grad_gate_h, grad_up_h, hidden], axis=1)
            trios.append(lax.all_gather(trio, "depth", axis=0, tiled=True))
            mixed = mixed + jnp.dot(hidden, wd, preferred_element_type=F32)
            grad_normed = grad_normed + contract_cols(grad_gate_h, wg) + contract_cols(grad_up_h, wu)
        for trio_all in trios:
            gates.append(contract_rows(normed_all, trio_all[:, :size]).astype(BF))
            ups.append(contract_rows(normed_all, trio_all[:, size:2 * size]).astype(BF))
            downs.append(contract_rows(trio_all[:, 2 * size:], cot_all).astype(BF))
        mixed = lax.psum_scatter(mixed.astype(BF), "col", scatter_dimension=0, tiled=True).astype(F32)
        output = (inputs + mixed).astype(BF)
        grad_normed = lax.psum_scatter(
            grad_normed.astype(BF), "col", scatter_dimension=0, tiled=True
        ).astype(F32)
        grad_scaled = grad_normed * norm_gain[None, :]
        proj = row_total(jnp.sum(grad_scaled * normal_rows, axis=1, keepdims=True))
        grad_tokens = (
            cotangent.astype(F32) + inv_rms * (grad_scaled - normal_rows * (proj / width))
        ).astype(BF)
        grad_gain = lax.psum(jnp.sum(grad_normed * normal_rows, axis=0), ("col", "depth"))
        return (
            output,
            grad_tokens,
            grad_gain,
            jnp.concatenate(gates, axis=1),
            jnp.concatenate(ups, axis=1),
            jnp.concatenate(downs, axis=0),
        )

    return body


MESH = pl.DeviceIdType.MESH


def exchange_kernel(n_col, chunks, size, width, tok_ref, gain_ref, cot_ref, wg_hbm, wu_hbm, wd_hbm,
                    mixed_ref, gn_ref, inv_ref, nall, call, gg_all, gu_all, h_all,
                    wg, wu, wd, both, sq_out, sq_in, part, peer, trio, acc_m, acc_g, end_out, end_in,
                    w_sem, sq_sem, ring_send, ring_recv, x_send, x_recv,
                    y_send, y_recv, c_send, c_recv, f_send, f_recv, l_sem,
                    ay_send, ay_recv, ac_send, ac_recv, af_send, af_recv, al_sem, e_send, e_recv):
    row, col, dep = lax.axis_index("row"), lax.axis_index("col"), lax.axis_index("depth")
    x_peer = {"row": 1 - row}
    me = lax.rem(dep, 2)
    y_peer = {"depth": lax.rem(dep + 2, 4)}
    c_peer = {"depth": dep + 1 - 2 * me}
    chip = pl.ds(dep - me, 2)
    y_chip = pl.ds(lax.rem(dep - me + 2, 4), 2)
    block = tok_ref.shape[0]
    has_left, has_right = col > 0, col < n_col - 1

    def cols_of(c):
        return pl.ds(pl.multiple_of((me * chunks + c) * size, size), size)

    def w_copies(c):
        return (
            pltpu.make_async_copy(wd_hbm.at[cols_of(c), :], wd.at[c], w_sem.at[c, 0]),
            pltpu.make_async_copy(wg_hbm.at[:, cols_of(c)], wg.at[c], w_sem.at[c, 1]),
            pltpu.make_async_copy(wu_hbm.at[:, cols_of(c)], wu.at[c], w_sem.at[c, 2]),
        )

    @pl.loop(0, chunks)
    def _(c):
        for copy in w_copies(c):
            copy.start()

    barrier = pltpu.get_barrier_semaphore()
    for peer_id in (x_peer, y_peer, c_peer):
        pl.semaphore_signal(barrier, inc=1, device_id=peer_id, device_id_type=MESH)

    @pl.when(has_left)
    def _():
        pl.semaphore_signal(barrier, inc=1, device_id={"col": col - 1}, device_id_type=MESH)

    @pl.when(has_right)
    def _():
        pl.semaphore_signal(barrier, inc=1, device_id={"col": col + 1}, device_id_type=MESH)

    own_rows = pl.ds(pl.multiple_of(col * block, block), block)
    both[1, me, own_rows, :] = cot_ref[...]
    inputs = tok_ref[...].astype(F32)
    sq_out[...] = jnp.broadcast_to(jnp.sum(inputs * inputs, axis=1, keepdims=True), sq_out.shape)
    pl.semaphore_wait(barrier, 3 + has_left.astype(jnp.int32) + has_right.astype(jnp.int32))
    sq_copy = pltpu.make_async_remote_copy(sq_out, sq_in, sq_sem.at[0], sq_sem.at[1], device_id=x_peer, device_id_type=MESH)
    sq_copy.start()

    def y_act(which, origin):
        rows = pl.ds(pl.multiple_of(origin * block, block), block)
        return pltpu.make_async_remote_copy(
            both.at[which, me, rows, :], (nall, call)[which].at[dep, rows, :],
            ay_send.at[which, origin], ay_recv.at[which, origin],
            device_id=y_peer, device_id_type=MESH)

    def hop(which, step, way):
        origin = col - step if way == 0 else col + step
        target = col + 1 if way == 0 else col - 1
        rows = pl.ds(pl.multiple_of(origin * block, block), block)
        return pltpu.make_async_remote_copy(
            both.at[which, me, rows, :], both.at[which, me, rows, :],
            ring_send.at[which, step, way], ring_recv.at[which, step, way],
            device_id={"col": target}, device_id_type=MESH)

    def sends(which, step, act):
        @pl.when((col - step >= 0) & has_right)
        def _():
            act(hop(which, step, 0))

        @pl.when((col + step < n_col) & has_left)
        def _():
            act(hop(which, step, 1))

    def arrive(which, step):
        @pl.when(col - 1 - step >= 0)
        def _():
            rows = pl.ds(pl.multiple_of((col - 1 - step) * block, block), block)
            pltpu.make_async_remote_copy(
                both.at[which, me, rows, :], both.at[which, me, rows, :],
                ring_send.at[which, step, 0], ring_recv.at[which, step, 0],
                device_id={"col": col - 1}, device_id_type=MESH).wait_recv()
            y_act(which, col - 1 - step).start()

        @pl.when(col + 1 + step < n_col)
        def _():
            rows = pl.ds(pl.multiple_of((col + 1 + step) * block, block), block)
            pltpu.make_async_remote_copy(
                both.at[which, me, rows, :], both.at[which, me, rows, :],
                ring_send.at[which, step, 1], ring_recv.at[which, step, 1],
                device_id={"col": col + 1}, device_id_type=MESH).wait_recv()
            y_act(which, col + 1 + step).start()

    sends(1, 0, lambda copy: copy.start())
    y_act(1, col).start()
    sq_copy.wait()
    inv = lax.rsqrt((sq_out[...] + sq_in[...]) / width + EPS)
    inv_ref[...] = inv
    both[0, me, own_rows, :] = (inputs * inv[:, :1] * gain_ref[...]).astype(BF)
    sends(0, 0, lambda copy: copy.start())
    y_act(0, col).start()
    for step in range(n_col - 1):
        for which in (1, 0):
            arrive(which, step)
            if step + 1 < n_col - 1:
                sends(which, step + 1, lambda copy: copy.start())
    for step in range(n_col - 1):
        for which in (1, 0):
            sends(which, step, lambda copy: copy.wait_send())

    def remote(src, dst, a, b, to):
        return pltpu.make_async_remote_copy(src, dst, a, b, device_id=to, device_id_type=MESH)

    def c_act(which):
        return remote(both.at[which, me], both.at[which, me], ac_send.at[which], ac_recv.at[which], c_peer)

    def own_act(which):
        return pltpu.make_async_copy(both.at[which], (nall, call)[which].at[chip], al_sem.at[which])

    def act_forward(which):
        ref = (nall, call)[which].at[lax.rem(dep + 2, 4)]
        return remote(ref, ref, af_send.at[which], af_recv.at[which], c_peer)

    for which in (1, 0):
        c_act(which).start()
    for which in (1, 0):
        c_act(which).wait()
        own_act(which).start()

    def x_copy(c):
        return remote(part.at[c], peer.at[c], x_send.at[c], x_recv.at[c], x_peer)

    @pl.loop(0, chunks)
    def _(c):
        for copy in w_copies(c):
            copy.wait()
        cot_rows = both[1].reshape(-1, both.shape[3])
        norm_rows = both[0].reshape(-1, both.shape[3])
        shape = part.shape[2:]
        part[c, 2] = contract_cols(cot_rows, wd[c]).astype(BF).reshape(shape)
        part[c, 0] = jnp.dot(norm_rows, wg[c], preferred_element_type=F32).astype(BF).reshape(shape)
        part[c, 1] = jnp.dot(norm_rows, wu[c], preferred_element_type=F32).astype(BF).reshape(shape)
        x_copy(c).start()

    outs = (gg_all, gu_all, h_all)

    def spread(c, k):
        dst = outs[k].at[chip, :, cols_of(c)]
        return (
            remote(trio.at[c, k], dst, y_send.at[c, k], y_recv.at[c, k], y_peer),
            remote(trio.at[c, k], dst, c_send.at[c, k], c_recv.at[c, k], c_peer),
            pltpu.make_async_copy(trio.at[c, k], dst, l_sem.at[c, k]),
        )

    def forward(c, k):
        ref = outs[k].at[y_chip, :, cols_of(c)]
        return remote(ref, ref, f_send.at[c, k], f_recv.at[c, k], c_peer)

    def pass_on(c):
        for k in range(3):
            spread(c, k)[0].wait_recv()
            forward(c, k).start()

    acc_m[...] = jnp.zeros_like(acc_m)
    acc_g[...] = jnp.zeros_like(acc_g)
    for which in (1, 0):
        for origin in range(n_col):
            y_act(which, origin).wait_recv()
        act_forward(which).start()

    @pl.loop(0, chunks)
    def _(c):
        x_copy(c).wait()
        gate = part[c, 0].astype(F32) + peer[c, 0].astype(F32)
        up = part[c, 1].astype(F32) + peer[c, 1].astype(F32)
        grad_hidden = part[c, 2].astype(F32) + peer[c, 2].astype(F32)
        sig = jax.nn.sigmoid(gate)
        act = gate * sig
        trio[c, 2] = (act * up).astype(BF)
        trio[c, 1] = (grad_hidden * act).astype(BF)
        trio[c, 0] = (grad_hidden * up * sig * (1.0 + gate * (1.0 - sig))).astype(BF)
        for k in range(3):
            for copy in spread(c, k):
                copy.start()
        flat = [trio[c, k].reshape(-1, size) for k in range(3)]
        shape = acc_m.shape
        acc_m[...] += jnp.dot(flat[2], wd[c], preferred_element_type=F32).reshape(shape)
        acc_g[...] += (contract_cols(flat[0], wg[c]) + contract_cols(flat[1], wu[c])).reshape(shape)

        @pl.when(c > 0)
        def _():
            pass_on(c - 1)

    def end_copy(k):
        return remote(end_out.at[k], end_in.at[k], e_send.at[k], e_recv.at[k], c_peer)

    end_out[0] = acc_m[1 - me].astype(BF)
    end_copy(0).start()
    end_out[1] = acc_g[1 - me].astype(BF)
    end_copy(1).start()
    pass_on(chunks - 1)
    for which in (1, 0):
        for origin in range(n_col):
            y_act(which, origin).wait_send()
        own_act(which).wait()
        act_forward(which).wait()
    end_copy(0).wait()
    mixed_ref[...] = (acc_m[me] + end_in[0].astype(F32)).astype(BF)
    end_copy(1).wait()
    gn_ref[...] = (acc_g[me] + end_in[1].astype(F32)).astype(BF)

    @pl.loop(0, chunks)
    def _(c):
        for k in range(3):
            y_one, c_one, l_one = spread(c, k)
            y_one.wait_send()
            c_one.wait()
            l_one.wait()
            forward(c, k).wait()


def exchange(mesh, tokens, norm_gain, cotangent, w_gate, w_up, w_down):
    n_col = mesh.shape["col"]
    block, feat = tokens.shape
    hidden = w_gate.shape[1]
    size = next(s for s in (256, 128) if hidden % (2 * s) == 0)
    chunks = hidden // (2 * size)
    rows = block * n_col
    sds = jax.ShapeDtypeStruct
    dma = pltpu.SemaphoreType.DMA
    vmem, hbm = pl.BlockSpec(memory_space=pltpu.VMEM), pl.BlockSpec(memory_space=pl.ANY)
    return pl.pallas_call(
        functools.partial(exchange_kernel, n_col, chunks, size, feat * 2),
        out_shape=[sds((rows, feat), BF)] * 2 + [sds((block, 128), F32)]
        + [sds((4, rows, feat), BF)] * 2 + [sds((4, rows, hidden), BF)] * 3,
        in_specs=[vmem] * 3 + [hbm] * 3,
        out_specs=[vmem] * 3 + [hbm] * 5,
        scratch_shapes=[
            pltpu.VMEM((chunks, feat, size), BF),
            pltpu.VMEM((chunks, feat, size), BF),
            pltpu.VMEM((chunks, size, feat), BF),
            pltpu.VMEM((2, 2, rows, feat), BF),
            pltpu.VMEM((block, 128), F32),
            pltpu.VMEM((block, 128), F32),
            pltpu.VMEM((chunks, 3, 2, rows, size), BF),
            pltpu.VMEM((chunks, 3, 2, rows, size), BF),
            pltpu.VMEM((chunks, 3, 2, rows, size), BF),
            pltpu.VMEM((2, rows, feat), F32),
            pltpu.VMEM((2, rows, feat), F32),
            pltpu.VMEM((2, rows, feat), BF),
            pltpu.VMEM((2, rows, feat), BF),
            dma((chunks, 3)), dma((2,)), dma((2, n_col, 2)), dma((2, n_col, 2)), dma((chunks,)), dma((chunks,)),
        ] + [dma((chunks, 3))] * 7 + [dma((2, n_col))] * 2 + [dma((2,))] * 7,
        compiler_params=pltpu.CompilerParams(
            collective_id=0, has_side_effects=True, vmem_limit_bytes=62 * 1024 * 1024
        ),
        cost_estimate=pl.CostEstimate(
            flops=12 * rows * feat * hidden, bytes_accessed=6 * feat * hidden + 24 * rows * hidden,
            transcendentals=rows * hidden),
    )(tokens, norm_gain[None, :], cotangent, w_gate, w_up, w_down)


def make_fused(mesh):
    n_col = mesh.shape["col"]

    def swap_add(value, axis, bit):
        count = mesh.shape[axis]
        return value + lax.ppermute(value, axis, [(i, i ^ bit) for i in range(count)])

    def body(tokens, norm_gain, w_gate, w_up, w_down, cotangent):
        width = tokens.shape[1] * 2
        mixed, grad_normed, inv, nall, call, gg_all, gu_all, h_all = exchange(
            mesh, tokens, norm_gain, cotangent, w_gate, w_up, w_down)
        mixed, grad_normed = (
            lax.psum_scatter(value, "col", scatter_dimension=0, tiled=True).astype(F32)
            for value in (mixed, grad_normed)
        )
        nall, call, gg_all, gu_all, h_all = (
            value.reshape(-1, value.shape[2]) for value in (nall, call, gg_all, gu_all, h_all))
        grad_gate = contract_rows(nall, gg_all).astype(BF)
        grad_up = contract_rows(nall, gu_all).astype(BF)
        grad_normed, grad_gate, grad_up, h_all, call = lax.optimization_barrier(
            (grad_normed, grad_gate, grad_up, h_all, call))
        grad_down = contract_rows(h_all, call).astype(BF)
        inputs = tokens.astype(F32)
        inv_rms = inv[:, :1]
        normal_rows = inputs * inv_rms
        output = (inputs + mixed).astype(BF)
        grad_scaled = grad_normed * norm_gain[None, :]
        proj = swap_add(jnp.sum(grad_scaled * normal_rows, axis=1, keepdims=True), "row", 1)
        grad_tokens = (
            cotangent.astype(F32) + inv_rms * (grad_scaled - normal_rows * (proj / width))
        ).astype(BF)
        grad_gain = jnp.sum(grad_normed * normal_rows, axis=0)
        for axis in ("depth", "col"):
            count = mesh.shape[axis]
            grad_gain = grad_gain + sum(
                lax.ppermute(grad_gain, axis, [(i, (i + step) % count) for i in range(count)])
                for step in range(1, count))
        return output, grad_tokens, grad_gain, grad_gate, grad_up, grad_down

    return body


def pick_body(mesh):
    shape = mesh.shape
    if shape["row"] == 2 and shape["depth"] == 4 and shape["col"] == 4:
        return make_fused(mesh)
    return make_body(mesh)


def solution(mesh):
    in_specs = (
        P(("col", "depth"), "row"),
        P("row"),
        P("row", "col"),
        P("row", "col"),
        P("col", "row"),
        P(("col", "depth"), "row"),
    )
    out_specs = (
        P(("col", "depth"), "row"),
        P(("col", "depth"), "row"),
        P("row"),
        P("row", "col"),
        P("row", "col"),
        P("col", "row"),
    )
    return jax.shard_map(
        pick_body(mesh), mesh=mesh, in_specs=in_specs, out_specs=out_specs, check_vma=False
    )
```
